1024 devices in a mesh: row: 16 (over z), col: 64 (over y, x, core).
Axes of the slice: x: 4, y: 8, z: 16, core: 2. Of those that a mesh axis runs over, the one named last changes fastest.
Arguments:
- left_tiles: float32 [128, 256, 512], P('row', 'col'), may hold values from 0.005 to 0.05
- left_index: int32 [16, 64, 4], P('row', 'col'), may hold values from 0 to 3, each once within a row
- left_count: int32 [16, 64], P('row', 'col'), may hold values from 1 to 4
- right_tiles: float32 [8192, 8192], P('row', 'col'), may hold values from 0.005 to 0.05
- right_index: int32 [16, 64], P('row', 'col'), may hold values from 0 to 15
Outputs:
- inflated: float32 [128, 8192], P('row', 'col')
The draws below stay inside these ranges and needn't reach their ends.
All inputs are finite; a program needn't handle non-finite values.
Results may differ from the reference program's by a relative error of at most 0.00005.
Values sent between devices are 32-bit elements; how exact they have to be, the bound alone decides.
A program may use at most 32 MiB of HBM per device.

```python
import math
import jax
import jax.numpy as jnp
from jax import lax

TILE = 512
SLOTS = 4
RB = 8
CB = 128
SPAN = 16
N_ROW = 16
N_COL = 64


def place_ends(result, own_key, smallest, top_value):
    shape = result.shape
    spot = [jax.random.randint(jax.random.fold_in(own_key, axis), (), 0, shape[axis]) for axis in range(len(shape))]
    result = result.at[tuple(spot)].set(smallest)
    longest = shape.index(max(shape))
    spot[longest] = (spot[longest] + 1) % shape[longest]
    return result.at[tuple(spot)].set(top_value)


def steps_of(rng, dims, shards, smallest, top_value):
    def one(dim, parts):
        heights = jax.random.uniform(jax.random.fold_in(jax.random.fold_in(rng, 6), dim), (parts,), jnp.float32, smallest / len(shards), top_value / len(shards))
        return jnp.repeat(jnp.exp(heights), dims[dim] // parts).reshape((-1,) + (1,) * (len(dims) - dim - 1))

    level = one(*shards[0])
    for cut in shards[1:]:
        level = level * one(*cut)
    return level


def setup_inputs(seed: int = 0) -> dict:
    seeds = jax.random.split(jax.random.key(seed), 6)
    left_tiles = jnp.clip(jnp.exp(math.log(0.05) - 2.3025851 * jax.random.uniform(seeds[0], (N_ROW * RB, N_COL * SLOTS, TILE), jnp.float32) ** steps_of(seeds[0], (N_ROW * RB, N_COL * SLOTS, TILE), ((0, 16), (1, 64)), -0.2, 0.2)), 0.005, 0.05)
    left_index = jax.vmap(lambda own: jax.random.permutation(own, SLOTS))(jax.random.split(seeds[1], N_ROW * N_COL)).reshape((N_ROW, N_COL, SLOTS)).astype(jnp.int32)
    left_count = place_ends(jax.random.randint(seeds[2], (N_ROW, N_COL), 1, SLOTS + 1), jax.random.fold_in(seeds[2], 1), 1, SLOTS).astype(jnp.int32)
    right_tiles = jnp.clip(jnp.exp(math.log(0.05) - 2.3025851 * jax.random.uniform(seeds[3], (N_ROW * TILE, N_COL * CB), jnp.float32) ** steps_of(seeds[3], (N_ROW * TILE, N_COL * CB), ((0, 16), (1, 64)), -0.2, 0.2)), 0.005, 0.05)
    right_index = place_ends(jax.random.randint(seeds[4], (N_ROW, N_COL), 0, SPAN), jax.random.fold_in(seeds[4], 1), 0, SPAN - 1).astype(jnp.int32)
    return {"left_tiles": left_tiles, "left_index": left_index, "left_count": left_count, "right_tiles": right_tiles, "right_index": right_index}


def reference(left_tiles, left_index, left_count, right_tiles, right_index):
    live = (jnp.arange(SLOTS).astype(jnp.int32)[None, None, :] < left_count[:, :, None]).astype(jnp.float32)
    strips = left_tiles.reshape(N_ROW, RB, N_COL, SLOTS, TILE) * live[:, None, :, :, None]
    onehot = (left_index[:, :, :, None] == jnp.arange(SLOTS).astype(jnp.int32)[None, None, None, :]).astype(jnp.float32)
    panel = jnp.einsum('rcsp,rbcst->rbcpt', onehot, strips, precision=lax.Precision.HIGHEST)
    panel = panel.reshape(N_ROW, RB, N_COL * SLOTS, TILE)
    global_ids = (jnp.arange(N_ROW).astype(jnp.int32)[:, None] * SPAN + right_index).astype(jnp.int32)
    rights = right_tiles.reshape(N_ROW, TILE, N_COL, CB)

    def one_block(row_panel):
        chosen = row_panel[:, global_ids, :]
        return jnp.einsum('bjct,jtcx->bcx', chosen, rights, precision=lax.Precision.HIGHEST)

    blocks = lax.map(one_block, panel)
    product = blocks.reshape(N_ROW * RB, N_COL * CB)
    squared = product * product
    colsum = jnp.sum(squared, axis=0, keepdims=True)
    return (N_ROW * RB) * squared / (colsum + 1e-6)
```

```python
import jax
import jax.numpy as jnp
from jax import lax
from jax.experimental import pallas as pl
from jax.experimental.pallas import tpu as pltpu
from jax.sharding import PartitionSpec as P

MESH = pl.DeviceIdType.MESH
NR, NC = 16, 64


def wait_for(ref, sem):
    pltpu.make_async_copy(ref, ref, sem).wait()


def kernel(
    left, left_index, left_count, right_hbm, right_index, out,
    right, strips, tiles, picked, panel, own_id, ids, ids_s, part, parts, col, cols,
    sem_right, sem_ids, s1, r1, si, ri, s2, r2, s3, r3, s4, r4,
):
    row, me = lax.axis_index("row"), lax.axis_index("col")
    barrier = pltpu.get_barrier_semaphore()

    def greet(r, c):
        pl.semaphore_signal(barrier, inc=1, device_id=(r, c), device_id_type=MESH)

    chunk, place = me // 16, lax.rem(me, 16)
    source_row = lax.rem(place, 4) * 4 + lax.rem(place // 4 + 3, 4)
    target_row, quarter = me // 4, lax.rem(me, 4)
    target_place = lax.rem(row + 1, 4) * 4 + row // 4
    for q in range(4):
        greet(source_row, row * 4 + q)

    def greet_plane(d, _):
        greet(row, lax.rem(me + d, NC))
        return 0

    def greet_line(d, _):
        greet(lax.rem(row + d, NR), me)
        return 0

    lax.fori_loop(1, NC, greet_plane, 0)
    lax.fori_loop(1, NR, greet_line, 0)
    fetch = pltpu.make_async_copy(right_hbm, right, sem_right)
    fetch.start()

    count = left_count[0, 0]
    for k in range(4):
        slot = [left[:, s, k * 128 : (k + 1) * 128] for s in range(4)]
        for t in range(4):
            total = jnp.zeros((8, 128), jnp.float32)
            for s in range(4):
                hit = jnp.logical_and(left_index[0, 0, s] == t, s < count)
                total = jnp.where(hit, slot[s], total)
            strips[k, t] = total
    own_id[...] = jnp.full((1, 128), right_index[0, 0], jnp.int32)
    pl.semaphore_wait(barrier, 4 + NC - 1 + NR - 1)

    def send_strips(k):
        return pltpu.make_async_remote_copy(
            src_ref=strips.at[k],
            dst_ref=tiles.at[pl.ds(quarter * 4, 4)],
            send_sem=s1,
            recv_sem=r1,
            device_id=(target_row, k * 16 + target_place),
            device_id_type=MESH,
        )

    for k in range(4):
        send_strips(k).start()

    def send_id(d, _):
        pltpu.make_async_remote_copy(
            src_ref=own_id,
            dst_ref=ids.at[me],
            send_sem=si,
            recv_sem=ri,
            device_id=(row, lax.rem(me + d, NC)),
            device_id_type=MESH,
        ).start()
        return 0

    lax.fori_loop(1, NC, send_id, 0)
    ids[me] = own_id[...]
    wait_for(ids.at[pl.ds(0, NC - 1)], ri)
    read = pltpu.make_async_copy(ids, ids_s, sem_ids)
    read.start()
    read.wait()
    wait_for(tiles, r1)

    slot_here = chunk * 16 + source_row

    def send_tile(d, _):
        c = lax.rem(me + d, NC)
        picked[d] = tiles[ids_s[c, 0, 0]]
        pltpu.make_async_remote_copy(
            src_ref=picked.at[d],
            dst_ref=panel.at[slot_here],
            send_sem=s2,
            recv_sem=r2,
            device_id=(row, c),
            device_id_type=MESH,
        ).start()
        return 0

    lax.fori_loop(1, NC, send_tile, 0)
    panel[slot_here] = tiles[ids_s[me, 0, 0]]
    fetch.wait()
    wait_for(panel.at[pl.ds(0, NC - 1)], r2)

    total = jnp.zeros((128, 128), jnp.float32)
    for k in range(4):
        a = panel[pl.ds(k * 16, 16)].reshape(128, 128)
        b = right[pl.ds(k * 128, 128), :]
        total += jnp.dot(a, b, precision=lax.Precision.HIGHEST, preferred_element_type=jnp.float32)
    part[...] = total.reshape(NR, 8, 128)

    def send_part(d, _):
        r = lax.rem(row + d, NR)
        pltpu.make_async_remote_copy(
            src_ref=part.at[r],
            dst_ref=parts.at[row],
            send_sem=s3,
            recv_sem=r3,
            device_id=(r, me),
            device_id_type=MESH,
        ).start()
        return 0

    lax.fori_loop(1, NR, send_part, 0)
    parts[row] = part[row]
    wait_for(parts.at[pl.ds(0, NR - 1)], r3)
    product = jnp.sum(parts[...], axis=0)
    squared = product * product
    col[...] = jnp.sum(squared, axis=0, keepdims=True)

    def send_col(d, _):
        pltpu.make_async_remote_copy(
            src_ref=col,
            dst_ref=cols.at[row],
            send_sem=s4,
            recv_sem=r4,
            device_id=(lax.rem(row + d, NR), me),
            device_id_type=MESH,
        ).start()
        return 0

    lax.fori_loop(1, NR, send_col, 0)
    cols[row] = col[...]
    wait_for(cols.at[pl.ds(0, NR - 1)], r4)
    colsum = jnp.sum(cols[...], axis=0)
    out[...] = 128.0 * squared / (colsum + 1e-06)

    wait_for(strips, s1)
    wait_for(ids.at[pl.ds(0, NC - 1)], si)
    wait_for(picked.at[pl.ds(1, NC - 1)], s2)
    wait_for(part.at[pl.ds(0, NR - 1)], s3)
    wait_for(cols.at[pl.ds(0, NR - 1)], s4)


def body(left_tiles, left_index, left_count, right_tiles, right_index):
    vmem, smem = (pl.BlockSpec(memory_space=m) for m in (pltpu.VMEM, pltpu.SMEM))
    f32, i32 = jnp.float32, jnp.int32
    return pl.pallas_call(
        kernel,
        out_shape=jax.ShapeDtypeStruct((8, 128), f32),
        in_specs=[vmem, smem, smem, pl.BlockSpec(memory_space=pl.ANY), smem],
        out_specs=vmem,
        scratch_shapes=[
            pltpu.VMEM((512, 128), f32),
            pltpu.VMEM((4, 4, 8, 128), f32),
            pltpu.VMEM((16, 8, 128), f32),
            pltpu.VMEM((NC, 8, 128), f32),
            pltpu.VMEM((NC, 8, 128), f32),
            pltpu.VMEM((1, 128), i32),
            pltpu.VMEM((NC, 1, 128), i32),
            pltpu.SMEM((NC, 1, 128), i32),
            pltpu.VMEM((NR, 8, 128), f32),
            pltpu.VMEM((NR, 8, 128), f32),
            pltpu.VMEM((1, 128), f32),
            pltpu.VMEM((NR, 1, 128), f32),
        ]
        + [pltpu.SemaphoreType.DMA] * 12,
        compiler_params=pltpu.CompilerParams(
            collective_id=0, has_side_effects=True, vmem_limit_bytes=56 << 20
        ),
    )(left_tiles, left_index, left_count, right_tiles, right_index)


def solution(mesh):
    return jax.shard_map(
        body,
        mesh=mesh,
        in_specs=(
            P("row", "col", None),
            P("row", "col", None),
            P("row", "col"),
            P("row", "col"),
            P("row", "col"),
        ),
        out_specs=P("row", "col"),
        check_vma=False,
    )
```

```python
import jax
import jax.numpy as jnp
from jax import lax
from jax.experimental import pallas as pl
from jax.experimental.pallas import tpu as pltpu
from jax.sharding import PartitionSpec as P

MESH = pl.DeviceIdType.MESH
NR, NC = 16, 64


def wait_for(ref, sem):
    pltpu.make_async_copy(ref, ref, sem).wait()


def kernel(
    left_hbm, index_hbm, count_hbm, right_hbm, own_hbm, out,
    left, left_index, left_count, right, right_index,
    strips, staged, tiles, picked, panel, own_id, ids, ids_s, part, near, half, far, result, mine,
    sem_left, sem_int, sem_right, sem_ids, s1, r1, s2, r2, si, ri, s3, r3, s4, r4, s5, r5, s6, r6,
):
    row, me = lax.axis_index("row"), lax.axis_index("col")
    barrier = pltpu.get_barrier_semaphore()

    def greet(r, c):
        pl.semaphore_signal(barrier, inc=1, device_id=(r, c), device_id_type=MESH)

    y, x, core = me // 8, lax.rem(me // 2, 4), lax.rem(me, 2)
    quarter = lax.rem(me, 4)
    offset = lax.rem(y - row // 2 + 8, 8)
    chunk = offset // 2
    source = (1 - x // 2) + 2 * lax.rem(x, 2) + 4 * core + 8 * lax.rem(offset, 2)
    parity = row // 8
    hold_x, hold_core = 2 * (1 - lax.rem(row, 2)) + lax.rem(row // 2, 2), lax.rem(row // 4, 2)

    def greet_line(d, _):
        greet(lax.rem(row + d, NR), me)
        return 0

    def greet_plane(d, _):
        greet(row, lax.rem(me + d, NC))
        return 0

    lax.fori_loop(1, NC, greet_plane, 0)
    for q in range(4):
        greet(source, y * 8 + lax.rem(row, 2) * 4 + q)
    lax.fori_loop(1, NR, greet_line, 0)

    ints = ((index_hbm, left_index), (count_hbm, left_count), (own_hbm, right_index))
    fetch_ints = [pltpu.make_async_copy(a, b, sem_int.at[i]) for i, (a, b) in enumerate(ints)]
    fetch_left = pltpu.make_async_copy(left_hbm, left, sem_left)
    fetch_right = pltpu.make_async_copy(right_hbm, right, sem_right)
    for fetch in fetch_ints:
        fetch.start()
    fetch_left.start()
    fetch_right.start()
    for fetch in fetch_ints:
        fetch.wait()
    fetch_left.wait()

    count = left_count[0, 0]
    for k in range(4):
        slot = [left[:, s, k * 128 : (k + 1) * 128] for s in range(4)]
        for t in range(4):
            total = jnp.zeros((8, 128), jnp.float32)
            for s in range(4):
                hit = jnp.logical_and(left_index[0, 0, s] == t, s < count)
                total = jnp.where(hit, slot[s], total)
            strips[k, t] = total
    own_id[...] = jnp.full((1, 128), right_index[0, 0], jnp.int32)
    pl.semaphore_wait(barrier, NC - 1 + 4 + NR - 1)

    def spread(k):
        return pltpu.make_async_remote_copy(
            src_ref=strips.at[k],
            dst_ref=staged.at[k],
            send_sem=s1.at[k],
            recv_sem=r1.at[k],
            device_id=(row, lax.rem(y + 2 * k + parity, 8) * 8 + lax.rem(me, 8)),
            device_id_type=MESH,
        )

    for k in range(1, 4):
        spread(k).start()
    pl.when(parity == 1)(lambda: spread(0).start())

    @pl.when(parity == 0)
    def _():
        staged[0] = strips[0]

    def send_id(d, _):
        pltpu.make_async_remote_copy(
            src_ref=own_id,
            dst_ref=ids.at[me],
            send_sem=si,
            recv_sem=ri,
            device_id=(row, lax.rem(me + d, NC)),
            device_id_type=MESH,
        ).start()
        return 0

    lax.fori_loop(1, NC, send_id, 0)
    ids[me] = own_id[...]

    def to_plane(k):
        plane = 2 * lax.rem(y - 2 * k - parity + 8, 8) + x // 2
        return pltpu.make_async_remote_copy(
            src_ref=staged.at[k],
            dst_ref=tiles.at[pl.ds(quarter * 4, 4)],
            send_sem=s2,
            recv_sem=r2,
            device_id=(plane, y * 8 + hold_x * 2 + hold_core),
            device_id_type=MESH,
        )

    pl.when(parity == 1)(lambda: spread(0).wait_recv())
    to_plane(0).start()
    for k in (1, 3, 2):
        spread(k).wait_recv()
        to_plane(k).start()
    wait_for(ids.at[pl.ds(0, NC - 1)], ri)
    read = pltpu.make_async_copy(ids, ids_s, sem_ids)
    read.start()
    read.wait()
    wait_for(tiles, r2)

    slot_here = chunk * 16 + source

    def send_tile(d, _):
        c = lax.rem(me + d, NC)
        picked[d] = tiles[ids_s[c, 0, 0]]
        pltpu.make_async_remote_copy(
            src_ref=picked.at[d],
            dst_ref=panel.at[slot_here],
            send_sem=s3,
            recv_sem=r3,
            device_id=(row, c),
            device_id_type=MESH,
        ).start()
        return 0

    lax.fori_loop(1, NC, send_tile, 0)
    panel[slot_here] = tiles[ids_s[me, 0, 0]]
    fetch_right.wait()
    wait_for(panel.at[pl.ds(0, NC - 1)], r3)

    total = jnp.zeros((128, 128), jnp.float32)
    for k in range(4):
        a = panel[pl.ds(k * 16, 16)].reshape(128, 128)
        b = right[pl.ds(k * 128, 128), :]
        total += jnp.dot(a, b, precision=lax.Precision.HIGHEST, preferred_element_type=jnp.float32)
    part[...] = total.reshape(4, 4, 8, 128)

    base, member = row // 4 * 4, lax.rem(row, 4)
    for d in range(1, 4):
        m = lax.rem(member + d, 4)
        pltpu.make_async_remote_copy(
            src_ref=part.at[m],
            dst_ref=near.at[member],
            send_sem=s4,
            recv_sem=r4,
            device_id=(base + m, me),
            device_id_type=MESH,
        ).start()
    near[member] = part[member]
    wait_for(near.at[pl.ds(0, 3)], r4)
    summed = near[0] + near[1] + near[2] + near[3]

    def give(r):
        return pltpu.make_async_remote_copy(
            src_ref=result.at[r],
            dst_ref=mine,
            send_sem=s6,
            recv_sem=r6,
            device_id=(r, me),
            device_id_type=MESH,
        )

    @pl.when(row != 0)
    def _():
        half[...] = summed
        copy = pltpu.make_async_remote_copy(
            src_ref=half,
            dst_ref=far.at[row],
            send_sem=s5,
            recv_sem=r5,
            device_id=(0, me),
            device_id_type=MESH,
        )
        copy.start()
        wait_for(mine, r6)
        out[...] = mine[...]
        copy.wait_send()

    @pl.when(row == 0)
    def _():
        far[0] = summed
        wait_for(far.at[pl.ds(0, NR - 1)], r5)
        product = jnp.sum(far[...].reshape(4, 16, 8, 128), axis=0)
        squared = product * product
        colsum = jnp.sum(jnp.sum(squared, axis=0), axis=0, keepdims=True)
        result[...] = 128.0 * squared / (colsum + 1e-06)[None]
        for r in range(1, NR):
            give(r).start()
        out[...] = result[0]
        wait_for(result.at[pl.ds(0, NR - 1)], s6)

    for k in range(1, 4):
        spread(k).wait_send()
    pl.when(parity == 1)(lambda: spread(0).wait_send())
    wait_for(tiles, s2)
    wait_for(ids.at[pl.ds(0, NC - 1)], si)
    wait_for(picked.at[pl.ds(1, NC - 1)], s3)
    wait_for(near.at[pl.ds(0, 3)], s4)


def body(left_tiles, left_index, left_count, right_tiles, right_index):
    f32, i32 = jnp.float32, jnp.int32
    dma = pltpu.SemaphoreType.DMA
    return pl.pallas_call(
        kernel,
        out_shape=jax.ShapeDtypeStruct((8, 128), f32),
        in_specs=[pl.BlockSpec(memory_space=pltpu.HBM)] * 5,
        out_specs=pl.BlockSpec(memory_space=pltpu.VMEM),
        scratch_shapes=[
            pltpu.VMEM((8, 4, 512), f32),
            pltpu.SMEM((1, 1, 4), i32),
            pltpu.SMEM((1, 1), i32),
            pltpu.VMEM((512, 128), f32),
            pltpu.SMEM((1, 1), i32),
            pltpu.VMEM((4, 4, 8, 128), f32),
            pltpu.VMEM((4, 4, 8, 128), f32),
            pltpu.VMEM((16, 8, 128), f32),
            pltpu.VMEM((NC, 8, 128), f32),
            pltpu.VMEM((NC, 8, 128), f32),
            pltpu.VMEM((1, 128), i32),
            pltpu.VMEM((NC, 1, 128), i32),
            pltpu.SMEM((NC, 1, 128), i32),
            pltpu.VMEM((4, 4, 8, 128), f32),
            pltpu.VMEM((4, 4, 8, 128), f32),
            pltpu.VMEM((4, 8, 128), f32),
            pltpu.VMEM((NR, 4, 8, 128), f32),
            pltpu.VMEM((NR, 8, 128), f32),
            pltpu.VMEM((8, 128), f32),
            dma, dma((3,)), dma, dma, dma((4,)), dma((4,)),
        ]
        + [dma] * 12,
        compiler_params=pltpu.CompilerParams(
            collective_id=0, has_side_effects=True, vmem_limit_bytes=56 << 20
        ),
    )(left_tiles, left_index, left_count, right_tiles, right_index)


def solution(mesh):
    return jax.shard_map(
        body,
        mesh=mesh,
        in_specs=(
            P("row", "col", None),
            P("row", "col", None),
            P("row", "col"),
            P("row", "col"),
            P("row", "col"),
        ),
        out_specs=P("row", "col"),
        check_vma=False,
    )
```

```python
import jax
import jax.numpy as jnp
from jax import lax
from jax.experimental import pallas as pl
from jax.experimental.pallas import tpu as pltpu
from jax.sharding import PartitionSpec as P

MESH = pl.DeviceIdType.MESH
NR, NC = 16, 64


def wait_for(ref, sem):
    pltpu.make_async_copy(ref, ref, sem).wait()


def kernel(
    left_hbm, index_hbm, count_hbm, right_hbm, own_hbm, out,
    left, left_index, left_count, right, right_index,
    strips, staged, tiles, picked, panel, own_id, ids, ids_s, part, near, half, far, result, mine,
    sem_left, sem_int, sem_right, sem_ids, s1, r1, s2, r2, si, ri, s3, r3, s4, r4, s5, r5, s6, r6, ready, plane_ready, near_ready,
):
    row, me = lax.axis_index("row"), lax.axis_index("col")
    barrier = pltpu.get_barrier_semaphore()

    def greet(r, c):
        pl.semaphore_signal(barrier, inc=1, device_id=(r, c), device_id_type=MESH)

    y, x, core = me // 8, lax.rem(me // 2, 4), lax.rem(me, 2)
    quarter = lax.rem(me, 4)
    offset = lax.rem(y - row // 2 + 8, 8)
    chunk = offset // 2
    source = (1 - x // 2) + 2 * lax.rem(x, 2) + 4 * core + 8 * lax.rem(offset, 2)
    parity = row // 8
    hold_x, hold_core = 2 * (1 - lax.rem(row, 2)) + lax.rem(row // 2, 2), lax.rem(row // 4, 2)

    planes = [2 * lax.rem(y - 2 * k - parity + 8, 8) + x // 2 for k in range(4)]
    above = [(p > row).astype(jnp.int32) for p in planes]
    below = [(p < row).astype(jnp.int32) for p in planes]
    n_above = above[0] + above[1] + above[2] + above[3]
    n_below = below[0] + below[1] + below[2] + below[3]
    member = lax.rem(row, 4)

    def on_line(d):
        return lax.rem(y + d, 8) * 8 + lax.rem(me, 8)

    def sender(q):
        return y * 8 + lax.rem(row, 2) * 4 + q

    def holder(k):
        return planes[k], y * 8 + hold_x * 2 + hold_core

    for d in range(1, 8):
        greet(row, on_line(d))
    for d in range(1, 8):
        greet(row, y * 8 + lax.rem(me + d, 8))

    @pl.when(source > row)
    def _():
        for q in range(4):
            greet(source, sender(q))

    for k in range(4):
        pl.when(planes[k] > row)(lambda k=k: greet(*holder(k)))
    for d in range(1, 4):
        pl.when(member + d < 4)(lambda d=d: greet(row + d, me))

    @pl.when(row == 0)
    def _():
        def greet_line(r, _):
            greet(r, me)
            return 0

        lax.fori_loop(4, NR, greet_line, 0)

    expected = 14 + 4 * (source < row).astype(jnp.int32) + n_below + member + (row >= 4).astype(jnp.int32)

    ints = ((index_hbm, left_index), (count_hbm, left_count), (own_hbm, right_index))
    fetch_ints = [pltpu.make_async_copy(a, b, sem_int.at[i]) for i, (a, b) in enumerate(ints)]
    fetch_left = pltpu.make_async_copy(left_hbm, left, sem_left)
    fetch_right = pltpu.make_async_copy(right_hbm, right, sem_right)
    for fetch in fetch_ints:
        fetch.start()
    fetch_left.start()
    fetch_right.start()
    for fetch in fetch_ints:
        fetch.wait()
    fetch_left.wait()

    count = left_count[0, 0]
    for k in range(4):
        slot = [left[:, s, k * 128 : (k + 1) * 128] for s in range(4)]
        for t in range(4):
            total = jnp.zeros((8, 128), jnp.float32)
            for s in range(4):
                hit = jnp.logical_and(left_index[0, 0, s] == t, s < count)
                total = jnp.where(hit, slot[s], total)
            strips[k, t] = total
    own_id[...] = jnp.full((1, 128), right_index[0, 0], jnp.int32)
    pl.semaphore_wait(barrier, expected)

    def spread(k):
        return pltpu.make_async_remote_copy(
            src_ref=strips.at[k],
            dst_ref=staged.at[k],
            send_sem=s1.at[k],
            recv_sem=r1.at[k],
            device_id=(row, on_line(2 * k + parity)),
            device_id_type=MESH,
        )

    for k in range(1, 4):
        spread(k).start()
    pl.when(parity == 1)(lambda: spread(0).start())

    @pl.when(parity == 0)
    def _():
        staged[0] = strips[0]

    def tell(sem, r, c):
        pl.semaphore_signal(sem, inc=1, device_id=(r, c), device_id_type=MESH)

    @pl.when(source < row)
    def _():
        for q in range(4):
            tell(ready, source, sender(q))

    for d in range(1, 8):
        tell(plane_ready, row, on_line(d))
    for d in range(1, 4):
        pl.when(member >= d)(lambda d=d: tell(near_ready, row - d, me))

    def to_plane(k):
        return pltpu.make_async_remote_copy(
            src_ref=staged.at[k],
            dst_ref=tiles.at[pl.ds(quarter * 4, 4)],
            send_sem=s2,
            recv_sem=r2,
            device_id=holder(k),
            device_id_type=MESH,
        )

    pl.when(parity == 1)(lambda: spread(0).wait_recv())
    pl.when(planes[0] <= row)(lambda: to_plane(0).start())
    for k in (1, 3, 2):
        spread(k).wait_recv()
        pl.when(planes[k] <= row)(lambda k=k: to_plane(k).start())

    def send_id(d, _):
        pltpu.make_async_remote_copy(
            src_ref=own_id,
            dst_ref=ids.at[me],
            send_sem=si,
            recv_sem=ri,
            device_id=(row, lax.rem(me + d, NC)),
            device_id_type=MESH,
        ).start()
        return 0

    pl.semaphore_wait(plane_ready, 7)
    lax.fori_loop(1, NC, send_id, 0)
    ids[me] = own_id[...]

    @pl.when(n_above > 0)
    def _():
        pl.semaphore_wait(ready, n_above)
        for k in range(4):
            pl.when(planes[k] > row)(lambda k=k: to_plane(k).start())

    wait_for(ids.at[pl.ds(0, NC - 1)], ri)
    read = pltpu.make_async_copy(ids, ids_s, sem_ids)
    read.start()
    read.wait()
    wait_for(tiles, r2)

    slot_here = chunk * 16 + source

    def send_tile(d, _):
        c = lax.rem(me + d, NC)
        picked[d] = tiles[ids_s[c, 0, 0]]
        pltpu.make_async_remote_copy(
            src_ref=picked.at[d],
            dst_ref=panel.at[slot_here],
            send_sem=s3,
            recv_sem=r3,
            device_id=(row, c),
            device_id_type=MESH,
        ).start()
        return 0

    lax.fori_loop(1, NC, send_tile, 0)
    panel[slot_here] = tiles[ids_s[me, 0, 0]]
    fetch_right.wait()
    wait_for(panel.at[pl.ds(0, NC - 1)], r3)

    total = jnp.zeros((128, 128), jnp.float32)
    for k in range(4):
        a = panel[pl.ds(k * 16, 16)].reshape(128, 128)
        b = right[pl.ds(k * 128, 128), :]
        total += jnp.dot(a, b, precision=lax.Precision.HIGHEST, preferred_element_type=jnp.float32)
    part[...] = total.reshape(2, 8, 8, 128)

    group = row // 4
    first = group * 4 + group // 2 * 2

    def gather_near(h):
        return pltpu.make_async_remote_copy(
            src_ref=part.at[h],
            dst_ref=near.at[member],
            send_sem=s4.at[h],
            recv_sem=r4,
            device_id=(first + h, me),
            device_id_type=MESH,
        )

    def give(r):
        return pltpu.make_async_remote_copy(
            src_ref=result.at[r],
            dst_ref=mine,
            send_sem=s6,
            recv_sem=r6,
            device_id=(r, me),
            device_id_type=MESH,
        )

    pl.when(member < 3)(lambda: pl.semaphore_wait(near_ready, 3 - member))
    for h in range(2):
        pl.when(row != first + h)(lambda h=h: gather_near(h).start())
    for h in range(2):

        @pl.when(row == first + h)
        def _(h=h):
            near[member] = part[h]
            wait_for(near.at[pl.ds(0, 3)], r4)
            half[...] = near[0] + near[1] + near[2] + near[3]

    gather_far = pltpu.make_async_remote_copy(
        src_ref=half,
        dst_ref=far.at[group * 2 + row - first],
        send_sem=s5,
        recv_sem=r5,
        device_id=(0, me),
        device_id_type=MESH,
    )
    holds = jnp.logical_and(row != 0, jnp.logical_or(row == first, row == first + 1))
    pl.when(holds)(lambda: gather_far.start())

    @pl.when(row != 0)
    def _():
        wait_for(mine, r6)
        out[...] = mine[...]

    @pl.when(row == 0)
    def _():
        far[0] = half[...]
        wait_for(far.at[pl.ds(0, 7)], r5)
        product = jnp.sum(far[...].reshape(4, 16, 8, 128), axis=0)
        squared = product * product
        colsum = jnp.sum(jnp.sum(squared, axis=0), axis=0, keepdims=True)
        result[...] = 128.0 * squared / (colsum + 1e-06)[None]
        for r in range(1, NR):
            give(r).start()
        out[...] = result[0]
        wait_for(result.at[pl.ds(0, NR - 1)], s6)

    pl.when(holds)(lambda: gather_far.wait_send())
    for h in range(2):
        pl.when(row != first + h)(lambda h=h: gather_near(h).wait_send())
    for k in range(1, 4):
        spread(k).wait_send()
    pl.when(parity == 1)(lambda: spread(0).wait_send())
    wait_for(tiles, s2)
    wait_for(ids.at[pl.ds(0, NC - 1)], si)
    wait_for(picked.at[pl.ds(1, NC - 1)], s3)


def body(left_tiles, left_index, left_count, right_tiles, right_index):
    f32, i32 = jnp.float32, jnp.int32
    dma = pltpu.SemaphoreType.DMA
    return pl.pallas_call(
        kernel,
        out_shape=jax.ShapeDtypeStruct((8, 128), f32),
        in_specs=[pl.BlockSpec(memory_space=pltpu.HBM)] * 5,
        out_specs=pl.BlockSpec(memory_space=pltpu.VMEM),
        scratch_shapes=[
            pltpu.VMEM((8, 4, 512), f32),
            pltpu.SMEM((1, 1, 4), i32),
            pltpu.SMEM((1, 1), i32),
            pltpu.VMEM((512, 128), f32),
            pltpu.SMEM((1, 1), i32),
            pltpu.VMEM((4, 4, 8, 128), f32),
            pltpu.VMEM((4, 4, 8, 128), f32),
            pltpu.VMEM((16, 8, 128), f32),
            pltpu.VMEM((NC, 8, 128), f32),
            pltpu.VMEM((NC, 8, 128), f32),
            pltpu.VMEM((1, 128), i32),
            pltpu.VMEM((NC, 1, 128), i32),
            pltpu.SMEM((NC, 1, 128), i32),
            pltpu.VMEM((2, 8, 8, 128), f32),
            pltpu.VMEM((4, 8, 8, 128), f32),
            pltpu.VMEM((8, 8, 128), f32),
            pltpu.VMEM((8, 8, 8, 128), f32),
            pltpu.VMEM((NR, 8, 128), f32),
            pltpu.VMEM((8, 128), f32),
            dma, dma((3,)), dma, dma, dma((4,)), dma((4,)),
        ]
        + [dma] * 6
        + [dma((2,))]
        + [dma] * 5
        + [pltpu.SemaphoreType.REGULAR] * 3,
        compiler_params=pltpu.CompilerParams(
            collective_id=0, has_side_effects=True, vmem_limit_bytes=56 << 20
        ),
    )(left_tiles, left_index, left_count, right_tiles, right_index)


def solution(mesh):
    return jax.shard_map(
        body,
        mesh=mesh,
        in_specs=(
            P("row", "col", None),
            P("row", "col", None),
            P("row", "col"),
            P("row", "col"),
            P("row", "col"),
        ),
        out_specs=P("row", "col"),
        check_vma=False,
    )
```

```python
import jax
import jax.numpy as jnp
from jax import lax
from jax.experimental import pallas as pl
from jax.experimental.pallas import tpu as pltpu
from jax.sharding import PartitionSpec as P

MESH = pl.DeviceIdType.MESH
NR, NC = 16, 64


def wait_for(ref, sem):
    pltpu.make_async_copy(ref, ref, sem).wait()


def kernel(
    left_hbm, index_hbm, count_hbm, right_hbm, own_hbm, out,
    left, left_index, left_count, right, right_index,
    strips, staged, tiles, picked, panel, own_id, ids, ids_s, part, near, half, far, result, mine,
    sem_left, sem_int, sem_right, sem_ids, s1, r1, s2, r2, si, ri, sj, rj, s3, r3, s4, r4, s5, r5, s6, r6, ready, plane_ready, near_ready,
):
    row, me = lax.axis_index("row"), lax.axis_index("col")
    barrier = pltpu.get_barrier_semaphore()

    def greet(r, c):
        pl.semaphore_signal(barrier, inc=1, device_id=(r, c), device_id_type=MESH)

    y, x, core = me // 8, lax.rem(me // 2, 4), lax.rem(me, 2)
    quarter = lax.rem(me, 4)
    offset = lax.rem(y - row // 2 + 8, 8)
    chunk = offset // 2
    source = x // 2 + 2 * lax.rem(x, 2) + 4 * core + 8 * lax.rem(offset, 2)
    parity = row // 8
    hold_x, hold_core = 2 * lax.rem(row, 2) + lax.rem(row // 2, 2), lax.rem(row // 4, 2)

    planes = [2 * lax.rem(y - 2 * k - parity + 8, 8) + x // 2 for k in range(4)]
    above = [(p > row).astype(jnp.int32) for p in planes]
    below = [(p < row).astype(jnp.int32) for p in planes]
    n_above = above[0] + above[1] + above[2] + above[3]
    n_below = below[0] + below[1] + below[2] + below[3]
    member = lax.rem(row, 4)

    def on_line(d):
        return lax.rem(y + d, 8) * 8 + lax.rem(me, 8)

    def sender(q):
        return y * 8 + lax.rem(row, 2) * 4 + q

    def holder(k):
        return planes[k], y * 8 + hold_x * 2 + hold_core

    for d in range(1, 8):
        greet(row, on_line(d))
    for d in range(1, 8):
        greet(row, y * 8 + lax.rem(me + d, 8))

    @pl.when(source > row)
    def _():
        for q in range(4):
            greet(source, sender(q))

    for k in range(4):
        pl.when(planes[k] > row)(lambda k=k: greet(*holder(k)))
    for d in range(1, 4):
        pl.when(member + d < 4)(lambda d=d: greet(row + d, me))

    @pl.when(row == 0)
    def _():
        def greet_line(r, _):
            greet(r, me)
            return 0

        lax.fori_loop(4, NR, greet_line, 0)

    expected = 14 + 4 * (source < row).astype(jnp.int32) + n_below + member + (row >= 4).astype(jnp.int32)

    ints = ((index_hbm, left_index), (count_hbm, left_count), (own_hbm, right_index))
    fetch_ints = [pltpu.make_async_copy(a, b, sem_int.at[i]) for i, (a, b) in enumerate(ints)]
    fetch_left = pltpu.make_async_copy(left_hbm, left, sem_left)
    fetch_right = pltpu.make_async_copy(right_hbm, right, sem_right)
    for fetch in fetch_ints:
        fetch.start()
    fetch_left.start()
    fetch_right.start()
    for fetch in fetch_ints:
        fetch.wait()
    fetch_left.wait()

    count = left_count[0, 0]
    for k in range(4):
        slot = [left[:, s, k * 128 : (k + 1) * 128] for s in range(4)]
        for t in range(4):
            total = jnp.zeros((8, 128), jnp.float32)
            for s in range(4):
                hit = jnp.logical_and(left_index[0, 0, s] == t, s < count)
                total = jnp.where(hit, slot[s], total)
            strips[k, t] = total
    own_id[...] = jnp.full((1, 128), right_index[0, 0], jnp.int32)
    pl.semaphore_wait(barrier, expected)

    def spread(k):
        return pltpu.make_async_remote_copy(
            src_ref=strips.at[k],
            dst_ref=staged.at[k],
            send_sem=s1.at[k],
            recv_sem=r1.at[k],
            device_id=(row, on_line(2 * k + parity)),
            device_id_type=MESH,
        )

    def tell(sem, r, c):
        pl.semaphore_signal(sem, inc=1, device_id=(r, c), device_id_type=MESH)

    @pl.when(source < row)
    def _():
        for q in range(4):
            tell(ready, source, sender(q))

    for k in range(1, 4):
        spread(k).start()
    pl.when(parity == 1)(lambda: spread(0).start())

    @pl.when(parity == 0)
    def _():
        staged[0] = strips[0]

    for d in range(1, 8):
        tell(plane_ready, row, on_line(d))
    for d in range(1, 4):
        pl.when(member >= d)(lambda d=d: tell(near_ready, row - d, me))

    def to_plane(k):
        return pltpu.make_async_remote_copy(
            src_ref=staged.at[k],
            dst_ref=tiles.at[pl.ds(quarter * 4, 4)],
            send_sem=s2.at[k],
            recv_sem=r2,
            device_id=holder(k),
            device_id_type=MESH,
        )

    here = jnp.logical_and(hold_x == x, hold_core == core)
    kept = [jnp.logical_and(here, planes[k] == row) for k in range(4)]
    sent = [jnp.logical_not(keep) for keep in kept]

    def keep_here(k):
        return pltpu.make_async_copy(staged.at[k], tiles.at[pl.ds(quarter * 4, 4)], r2)

    def pass_on(k):
        pl.when(jnp.logical_and(sent[k], planes[k] <= row))(lambda: to_plane(k).start())
        pl.when(kept[k])(lambda: keep_here(k).start())

    def send_id(d):
        return pltpu.make_async_remote_copy(
            src_ref=own_id,
            dst_ref=ids.at[y, lax.rem(me, 8)],
            send_sem=si,
            recv_sem=ri,
            device_id=(row, y * 8 + lax.rem(me + d, 8)),
            device_id_type=MESH,
        )

    def send_ids(d):
        return pltpu.make_async_remote_copy(
            src_ref=ids.at[y],
            dst_ref=ids.at[y],
            send_sem=sj,
            recv_sem=rj,
            device_id=(row, on_line(d)),
            device_id_type=MESH,
        )

    for d in range(1, 8):
        send_id(d).start()
    ids[y, lax.rem(me, 8)] = own_id[...]
    pl.when(parity == 1)(lambda: spread(0).wait_recv())
    pass_on(0)
    wait_for(ids.at[0, pl.ds(0, 7)], ri)
    for d in range(1, 8):
        send_ids(d).start()
    for k in (1, 3, 2):
        spread(k).wait_recv()
        pass_on(k)

    @pl.when(n_above > 0)
    def _():
        pl.semaphore_wait(ready, n_above)
        for k in range(4):
            pl.when(planes[k] > row)(lambda k=k: to_plane(k).start())

    wait_for(ids.at[pl.ds(0, 7)], rj)
    read = pltpu.make_async_copy(ids, ids_s, sem_ids)
    read.start()
    read.wait()
    wait_for(tiles, r2)
    pl.semaphore_wait(plane_ready, 7)

    slot_here = chunk * 16 + source

    def send_tile(c, d):
        picked[d] = tiles[ids_s[c // 8, lax.rem(c, 8), 0, 0]]
        pltpu.make_async_remote_copy(
            src_ref=picked.at[d],
            dst_ref=panel.at[slot_here],
            send_sem=s3,
            recv_sem=r3.at[source // 8],
            device_id=(row, c),
            device_id_type=MESH,
        ).start()

    for n, d in enumerate((4, 3, 5, 2, 6, 1, 7, 0)):

        def send_group(i, _, n=n, d=d):
            send_tile(lax.rem(y + d, 8) * 8 + lax.rem(me + i, 8), (7 - n) * 8 + i)
            return 0

        lax.fori_loop(0 if d else 1, 8, send_group, 0)

    panel[slot_here] = tiles[ids_s[y, lax.rem(me, 8), 0, 0]]
    fetch_right.wait()

    group = row // 4
    first = group * 4 + group // 2 * 2

    def gather_near(h):
        return pltpu.make_async_remote_copy(
            src_ref=part.at[h],
            dst_ref=near.at[member],
            send_sem=s4.at[h],
            recv_sem=r4,
            device_id=(first + h, me),
            device_id_type=MESH,
        )

    def give(r):
        return pltpu.make_async_remote_copy(
            src_ref=result.at[r],
            dst_ref=mine,
            send_sem=s6,
            recv_sem=r6,
            device_id=(r, me),
            device_id_type=MESH,
        )

    def multiply(h):
        pl.when(source // 8 == h)(lambda: wait_for(panel.at[pl.ds(0, 31)], r3.at[h]))
        pl.when(source // 8 != h)(lambda: wait_for(panel.at[pl.ds(0, 32)], r3.at[h]))
        total = jnp.zeros((64, 128), jnp.float32)
        for k in range(4):
            a = panel[pl.ds(k * 16 + h * 8, 8)].reshape(64, 128)
            b = right[pl.ds(k * 128, 128), :]
            total += jnp.dot(a, b, precision=lax.Precision.HIGHEST, preferred_element_type=jnp.float32)
        part[h] = total.reshape(8, 8, 128)
        pl.when(row != first + h)(lambda: gather_near(h).start())

        @pl.when(row == first + h)
        def _():
            near[member] = part[h]

    pl.when(member < 3)(lambda: pl.semaphore_wait(near_ready, 3 - member))
    own_half = row // 8
    multiply(own_half)
    multiply(1 - own_half)
    for h in range(2):

        @pl.when(row == first + h)
        def _(h=h):
            wait_for(near.at[pl.ds(0, 3)], r4)
            half[...] = near[0] + near[1] + near[2] + near[3]

    gather_far = pltpu.make_async_remote_copy(
        src_ref=half,
        dst_ref=far.at[group * 2 + row - first],
        send_sem=s5,
        recv_sem=r5,
        device_id=(0, me),
        device_id_type=MESH,
    )
    holds = jnp.logical_and(row != 0, jnp.logical_or(row == first, row == first + 1))
    pl.when(holds)(lambda: gather_far.start())

    @pl.when(row != 0)
    def _():
        wait_for(mine, r6)
        out[...] = mine[...]

    @pl.when(row == 0)
    def _():
        far[0] = half[...]
        wait_for(far.at[pl.ds(0, 7)], r5)
        product = jnp.sum(far[...].reshape(4, 16, 8, 128), axis=0)
        squared = product * product
        colsum = jnp.sum(jnp.sum(squared, axis=0), axis=0, keepdims=True)
        result[...] = squared * (128.0 / (colsum + 1e-06))[None]
        for r in range(1, NR):
            give(r).start()
        out[...] = result[0]
        wait_for(result.at[pl.ds(0, NR - 1)], s6)

    pl.when(holds)(lambda: gather_far.wait_send())
    for h in range(2):
        pl.when(row != first + h)(lambda h=h: gather_near(h).wait_send())
    for k in range(1, 4):
        spread(k).wait_send()
    pl.when(parity == 1)(lambda: spread(0).wait_send())
    for k in range(4):
        pl.when(sent[k])(lambda k=k: to_plane(k).wait_send())
    wait_for(ids.at[0, pl.ds(0, 7)], si)
    wait_for(ids.at[pl.ds(0, 7)], sj)
    wait_for(picked.at[pl.ds(1, NC - 1)], s3)


def body(left_tiles, left_index, left_count, right_tiles, right_index):
    f32, i32 = jnp.float32, jnp.int32
    dma = pltpu.SemaphoreType.DMA
    return pl.pallas_call(
        kernel,
        out_shape=jax.ShapeDtypeStruct((8, 128), f32),
        in_specs=[pl.BlockSpec(memory_space=pltpu.HBM)] * 5,
        out_specs=pl.BlockSpec(memory_space=pltpu.VMEM),
        scratch_shapes=[
            pltpu.VMEM((8, 4, 512), f32),
            pltpu.SMEM((1, 1, 4), i32),
            pltpu.SMEM((1, 1), i32),
            pltpu.VMEM((512, 128), f32),
            pltpu.SMEM((1, 1), i32),
            pltpu.VMEM((4, 4, 8, 128), f32),
            pltpu.VMEM((4, 4, 8, 128), f32),
            pltpu.VMEM((16, 8, 128), f32),
            pltpu.VMEM((NC, 8, 128), f32),
            pltpu.VMEM((NC, 8, 128), f32),
            pltpu.VMEM((1, 128), i32),
            pltpu.VMEM((8, 8, 1, 128), i32),
            pltpu.SMEM((8, 8, 1, 128), i32),
            pltpu.VMEM((2, 8, 8, 128), f32),
            pltpu.VMEM((4, 8, 8, 128), f32),
            pltpu.VMEM((8, 8, 128), f32),
            pltpu.VMEM((8, 8, 8, 128), f32),
            pltpu.VMEM((NR, 8, 128), f32),
            pltpu.VMEM((8, 128), f32),
            dma, dma((3,)), dma, dma, dma((4,)), dma((4,)), dma((4,)),
        ]
        + [dma] * 6
        + [dma((2,)), dma((2,))]
        + [dma] * 5
        + [pltpu.SemaphoreType.REGULAR] * 3,
        compiler_params=pltpu.CompilerParams(
            collective_id=0, has_side_effects=True, vmem_limit_bytes=56 << 20
        ),
    )(left_tiles, left_index, left_count, right_tiles, right_index)


def solution(mesh):
    return jax.shard_map(
        body,
        mesh=mesh,
        in_specs=(
            P("row", "col", None),
            P("row", "col", None),
            P("row", "col"),
            P("row", "col"),
            P("row", "col"),
        ),
        out_specs=P("row", "col"),
        check_vma=False,
    )
```

```python
import jax
import jax.numpy as jnp
from jax import lax
from jax.experimental import pallas as pl
from jax.experimental.pallas import tpu as pltpu
from jax.sharding import PartitionSpec as P

MESH = pl.DeviceIdType.MESH
NR, NC = 16, 64


def wait_for(ref, sem):
    pltpu.make_async_copy(ref, ref, sem).wait()


def kernel(
    left_hbm, index_hbm, count_hbm, right_hbm, own_hbm, out,
    left, left_index, left_count, right, right_index,
    strips, staged, tiles, picked, panel, own_id, ids, ids_s, part, near, half, far, result, mine,
    sem_left, sem_int, sem_right, sem_ids, s1, r1, s2, r2, si, ri, sj, rj, s3, r3, s4, r4, s5, r5, s6, r6, ready, plane_ready, near_ready,
):
    row, me = lax.axis_index("row"), lax.axis_index("col")
    barrier = pltpu.get_barrier_semaphore()

    def greet(r, c):
        pl.semaphore_signal(barrier, inc=1, device_id=(r, c), device_id_type=MESH)

    y, x, core = me // 8, lax.rem(me // 2, 4), lax.rem(me, 2)
    quarter = lax.rem(me, 4)
    offset = lax.rem(y - row // 2 + 8, 8)
    chunk = offset // 2
    source = x // 2 + 2 * lax.rem(x, 2) + 4 * core + 8 * lax.rem(offset, 2)
    parity = row // 8
    hold_x, hold_core = 2 * lax.rem(row, 2) + lax.rem(row // 2, 2), lax.rem(row // 4, 2)

    planes = [2 * lax.rem(y - 2 * k - parity + 8, 8) + x // 2 for k in range(4)]
    above = [(p > row).astype(jnp.int32) for p in planes]
    below = [(p < row).astype(jnp.int32) for p in planes]
    n_above = above[0] + above[1] + above[2] + above[3]
    n_below = below[0] + below[1] + below[2] + below[3]
    member = lax.rem(row, 4)

    def on_line(d):
        return lax.rem(y + d, 8) * 8 + lax.rem(me, 8)

    def sender(q):
        return y * 8 + lax.rem(row, 2) * 4 + q

    def holder(k):
        return planes[k], y * 8 + hold_x * 2 + hold_core

    for d in range(1, 8):
        greet(row, on_line(d))
    for d in range(1, 8):
        greet(row, y * 8 + lax.rem(me + d, 8))

    @pl.when(source > row)
    def _():
        for q in range(4):
            greet(source, sender(q))

    for k in range(4):
        pl.when(planes[k] > row)(lambda k=k: greet(*holder(k)))
    for d in range(1, 4):
        pl.when(member + d < 4)(lambda d=d: greet(row + d, me))

    @pl.when(row == 0)
    def _():
        def greet_line(r, _):
            greet(r, me)
            return 0

        lax.fori_loop(4, NR, greet_line, 0)

    expected = 14 + 4 * (source < row).astype(jnp.int32) + n_below + member + (row >= 4).astype(jnp.int32)

    ints = ((index_hbm, left_index), (count_hbm, left_count), (own_hbm, right_index))
    fetch_ints = [pltpu.make_async_copy(a, b, sem_int.at[i]) for i, (a, b) in enumerate(ints)]
    fetch_left = pltpu.make_async_copy(left_hbm, left, sem_left)
    fetch_right = pltpu.make_async_copy(right_hbm, right, sem_right)
    for fetch in fetch_ints:
        fetch.start()
    fetch_left.start()
    fetch_right.start()
    for fetch in fetch_ints:
        fetch.wait()
    fetch_left.wait()

    count = left_count[0, 0]
    for k in range(4):
        slot = [left[:, s, k * 128 : (k + 1) * 128] for s in range(4)]
        for t in range(4):
            total = jnp.zeros((8, 128), jnp.float32)
            for s in range(4):
                hit = jnp.logical_and(left_index[0, 0, s] == t, s < count)
                total = jnp.where(hit, slot[s], total)
            strips[k, t] = total
    own_id[...] = jnp.full((1, 128), right_index[0, 0], jnp.int32)
    pl.semaphore_wait(barrier, expected)

    def spread(k):
        return pltpu.make_async_remote_copy(
            src_ref=strips.at[k],
            dst_ref=staged.at[k],
            send_sem=s1.at[k],
            recv_sem=r1.at[k],
            device_id=(row, on_line(2 * k + parity)),
            device_id_type=MESH,
        )

    def tell(sem, r, c):
        pl.semaphore_signal(sem, inc=1, device_id=(r, c), device_id_type=MESH)

    @pl.when(source < row)
    def _():
        for q in range(4):
            tell(ready, source, sender(q))

    for k in range(1, 4):
        spread(k).start()
    pl.when(parity == 1)(lambda: spread(0).start())

    @pl.when(parity == 0)
    def _():
        staged[0] = strips[0]

    for d in range(1, 8):
        tell(plane_ready, row, on_line(d))
    for d in range(1, 4):
        pl.when(member >= d)(lambda d=d: tell(near_ready, row - d, me))

    def to_plane(k):
        return pltpu.make_async_remote_copy(
            src_ref=staged.at[k],
            dst_ref=tiles.at[pl.ds(quarter * 4, 4)],
            send_sem=s2.at[k],
            recv_sem=r2,
            device_id=holder(k),
            device_id_type=MESH,
        )

    here = jnp.logical_and(hold_x == x, hold_core == core)
    kept = [jnp.logical_and(here, planes[k] == row) for k in range(4)]
    sent = [jnp.logical_not(keep) for keep in kept]

    def keep_here(k):
        return pltpu.make_async_copy(staged.at[k], tiles.at[pl.ds(quarter * 4, 4)], r2)

    def pass_on(k):
        pl.when(jnp.logical_and(sent[k], planes[k] <= row))(lambda: to_plane(k).start())
        pl.when(kept[k])(lambda: keep_here(k).start())

    def send_id(d):
        return pltpu.make_async_remote_copy(
            src_ref=own_id,
            dst_ref=ids.at[y, lax.rem(me, 8)],
            send_sem=si,
            recv_sem=ri,
            device_id=(row, y * 8 + lax.rem(me + d, 8)),
            device_id_type=MESH,
        )

    def send_ids(d):
        return pltpu.make_async_remote_copy(
            src_ref=ids.at[y],
            dst_ref=ids.at[y],
            send_sem=sj,
            recv_sem=rj,
            device_id=(row, on_line(d)),
            device_id_type=MESH,
        )

    for d in range(1, 8):
        send_id(d).start()
    ids[y, lax.rem(me, 8)] = own_id[...]
    pl.when(parity == 1)(lambda: spread(0).wait_recv())
    pass_on(0)
    wait_for(ids.at[0, pl.ds(0, 7)], ri)
    for d in range(1, 8):
        send_ids(d).start()
    for k in (1, 3, 2):
        spread(k).wait_recv()
        pass_on(k)

    @pl.when(n_above > 0)
    def _():
        pl.semaphore_wait(ready, n_above)
        for k in range(4):
            pl.when(planes[k] > row)(lambda k=k: to_plane(k).start())

    wait_for(ids.at[pl.ds(0, 7)], rj)
    read = pltpu.make_async_copy(ids, ids_s, sem_ids)
    read.start()
    read.wait()
    wait_for(tiles, r2)
    pl.semaphore_wait(plane_ready, 7)

    slot_here = chunk * 16 + source

    def send_tile(c, d):
        picked[d] = tiles[ids_s[c // 8, lax.rem(c, 8), 0, 0]]
        pltpu.make_async_remote_copy(
            src_ref=picked.at[d],
            dst_ref=panel.at[slot_here],
            send_sem=s3,
            recv_sem=r3.at[source // 8],
            device_id=(row, c),
            device_id_type=MESH,
        ).start()

    for n in range(16):
        to_core, d = n // 8, (4, 3, 5, 2, 6, 1, 7, 0)[n % 8]

        def send_group(i, _, n=n, to_core=to_core, d=d):
            c = lax.rem(y + d, 8) * 8 + 2 * lax.rem(x + i, 4) + to_core
            pl.when(c != me)(lambda: send_tile(c, n * 4 + i))
            return 0

        lax.fori_loop(0, 4, send_group, 0)

    panel[slot_here] = tiles[ids_s[y, lax.rem(me, 8), 0, 0]]
    fetch_right.wait()

    group = row // 4
    first = group * 4 + group // 2 * 2

    def gather_near(h):
        return pltpu.make_async_remote_copy(
            src_ref=part.at[h],
            dst_ref=near.at[member],
            send_sem=s4.at[h],
            recv_sem=r4,
            device_id=(first + h, me),
            device_id_type=MESH,
        )

    def give(r):
        return pltpu.make_async_remote_copy(
            src_ref=result.at[r],
            dst_ref=mine,
            send_sem=s6,
            recv_sem=r6,
            device_id=(r, me),
            device_id_type=MESH,
        )

    def multiply(h):
        pl.when(source // 8 == h)(lambda: wait_for(panel.at[pl.ds(0, 31)], r3.at[h]))
        pl.when(source // 8 != h)(lambda: wait_for(panel.at[pl.ds(0, 32)], r3.at[h]))
        total = jnp.zeros((64, 128), jnp.float32)
        for k in range(4):
            a = panel[pl.ds(k * 16 + h * 8, 8)].reshape(64, 128)
            b = right[pl.ds(k * 128, 128), :]
            total += jnp.dot(a, b, precision=lax.Precision.HIGHEST, preferred_element_type=jnp.float32)
        part[h] = total.reshape(8, 8, 128)
        pl.when(row != first + h)(lambda: gather_near(h).start())

        @pl.when(row == first + h)
        def _():
            near[member] = part[h]

    pl.when(member < 3)(lambda: pl.semaphore_wait(near_ready, 3 - member))
    own_half = row // 8
    multiply(own_half)
    multiply(1 - own_half)
    for h in range(2):

        @pl.when(row == first + h)
        def _(h=h):
            wait_for(near.at[pl.ds(0, 3)], r4)
            half[...] = near[0] + near[1] + near[2] + near[3]

    gather_far = pltpu.make_async_remote_copy(
        src_ref=half,
        dst_ref=far.at[group * 2 + row - first],
        send_sem=s5,
        recv_sem=r5,
        device_id=(0, me),
        device_id_type=MESH,
    )
    holds = jnp.logical_and(row != 0, jnp.logical_or(row == first, row == first + 1))
    pl.when(holds)(lambda: gather_far.start())

    @pl.when(row != 0)
    def _():
        wait_for(mine, r6)
        out[...] = mine[...]

    @pl.when(row == 0)
    def _():
        far[0] = half[...]
        wait_for(far.at[pl.ds(0, 7)], r5)
        product = jnp.sum(far[...].reshape(4, 16, 8, 128), axis=0)
        squared = product * product
        colsum = jnp.sum(jnp.sum(squared, axis=0), axis=0, keepdims=True)
        result[...] = squared * (128.0 / (colsum + 1e-06))[None]
        for r in range(1, NR):
            give(r).start()
        out[...] = result[0]
        wait_for(result.at[pl.ds(0, NR - 1)], s6)

    pl.when(holds)(lambda: gather_far.wait_send())
    for h in range(2):
        pl.when(row != first + h)(lambda h=h: gather_near(h).wait_send())
    for k in range(1, 4):
        spread(k).wait_send()
    pl.when(parity == 1)(lambda: spread(0).wait_send())
    for k in range(4):
        pl.when(sent[k])(lambda k=k: to_plane(k).wait_send())
    wait_for(ids.at[0, pl.ds(0, 7)], si)
    wait_for(ids.at[pl.ds(0, 7)], sj)
    wait_for(picked.at[pl.ds(1, NC - 1)], s3)


def body(left_tiles, left_index, left_count, right_tiles, right_index):
    f32, i32 = jnp.float32, jnp.int32
    dma = pltpu.SemaphoreType.DMA
    return pl.pallas_call(
        kernel,
        out_shape=jax.ShapeDtypeStruct((8, 128), f32),
        in_specs=[pl.BlockSpec(memory_space=pltpu.HBM)] * 5,
        out_specs=pl.BlockSpec(memory_space=pltpu.VMEM),
        scratch_shapes=[
            pltpu.VMEM((8, 4, 512), f32),
            pltpu.SMEM((1, 1, 4), i32),
            pltpu.SMEM((1, 1), i32),
            pltpu.VMEM((512, 128), f32),
            pltpu.SMEM((1, 1), i32),
            pltpu.VMEM((4, 4, 8, 128), f32),
            pltpu.VMEM((4, 4, 8, 128), f32),
            pltpu.VMEM((16, 8, 128), f32),
            pltpu.VMEM((NC, 8, 128), f32),
            pltpu.VMEM((NC, 8, 128), f32),
            pltpu.VMEM((1, 128), i32),
            pltpu.VMEM((8, 8, 1, 128), i32),
            pltpu.SMEM((8, 8, 1, 128), i32),
            pltpu.VMEM((2, 8, 8, 128), f32),
            pltpu.VMEM((4, 8, 8, 128), f32),
            pltpu.VMEM((8, 8, 128), f32),
            pltpu.VMEM((8, 8, 8, 128), f32),
            pltpu.VMEM((NR, 8, 128), f32),
            pltpu.VMEM((8, 128), f32),
            dma, dma((3,)), dma, dma, dma((4,)), dma((4,)), dma((4,)),
        ]
        + [dma] * 6
        + [dma((2,)), dma((2,))]
        + [dma] * 5
        + [pltpu.SemaphoreType.REGULAR] * 3,
        compiler_params=pltpu.CompilerParams(
            collective_id=0, has_side_effects=True, vmem_limit_bytes=56 << 20
        ),
    )(left_tiles, left_index, left_count, right_tiles, right_index)


def solution(mesh):
    return jax.shard_map(
        body,
        mesh=mesh,
        in_specs=(
            P("row", "col", None),
            P("row", "col", None),
            P("row", "col"),
            P("row", "col"),
            P("row", "col"),
        ),
        out_specs=P("row", "col"),
        check_vma=False,
    )
```

```python
import jax
import jax.numpy as jnp
from jax import lax
from jax.experimental import pallas as pl
from jax.experimental.pallas import tpu as pltpu
from jax.sharding import PartitionSpec as P

MESH = pl.DeviceIdType.MESH
NR, NC = 16, 64


def wait_for(ref, sem):
    pltpu.make_async_copy(ref, ref, sem).wait()


def kernel(
    left_hbm, index_hbm, count_hbm, right_hbm, own_hbm, out,
    left, left_index, left_count, right, right_index,
    strips, staged, tiles, picked, panel, own_id, ids, ids_s, part, near, half, far, result, mine,
    sem_left, sem_int, sem_right, sem_ids, s1, r1, s2, r2, si, ri, sj, rj, s3, r3, s4, r4, s5, r5, s6, r6, ready, plane_ready, near_ready,
):
    row, me = lax.axis_index("row"), lax.axis_index("col")
    barrier = pltpu.get_barrier_semaphore()

    def greet(r, c):
        pl.semaphore_signal(barrier, inc=1, device_id=(r, c), device_id_type=MESH)

    ints = ((index_hbm, left_index), (count_hbm, left_count), (own_hbm, right_index))
    fetch_ints = [pltpu.make_async_copy(a, b, sem_int.at[i]) for i, (a, b) in enumerate(ints)]
    fetch_left = pltpu.make_async_copy(left_hbm, left, sem_left)
    fetch_right = pltpu.make_async_copy(right_hbm, right, sem_right)
    for fetch in fetch_ints:
        fetch.start()
    fetch_left.start()
    fetch_right.start()

    y, x, core = me // 8, lax.rem(me // 2, 4), lax.rem(me, 2)
    quarter = lax.rem(me, 4)
    offset = lax.rem(y - row // 2 + 8, 8)
    chunk = offset // 2
    source = x // 2 + 2 * lax.rem(x, 2) + 4 * core + 8 * lax.rem(offset, 2)
    parity = row // 8
    hold_x, hold_core = 2 * lax.rem(row, 2) + lax.rem(row // 2, 2), lax.rem(row // 4, 2)

    planes = [2 * lax.rem(y - 2 * k - parity + 8, 8) + x // 2 for k in range(4)]
    above = [(p > row).astype(jnp.int32) for p in planes]
    below = [(p < row).astype(jnp.int32) for p in planes]
    n_above = above[0] + above[1] + above[2] + above[3]
    n_below = below[0] + below[1] + below[2] + below[3]
    member = lax.rem(row, 4)

    def on_line(d):
        return lax.rem(y + d, 8) * 8 + lax.rem(me, 8)

    def sender(q):
        return y * 8 + lax.rem(row, 2) * 4 + q

    def holder(k):
        return planes[k], y * 8 + hold_x * 2 + hold_core

    for d in range(1, 8):
        greet(row, on_line(d))
    for d in range(1, 8):
        greet(row, y * 8 + lax.rem(me + d, 8))

    @pl.when(source > row)
    def _():
        for q in range(4):
            greet(source, sender(q))

    for k in range(4):
        pl.when(planes[k] > row)(lambda k=k: greet(*holder(k)))
    for d in range(1, 4):
        pl.when(member + d < 4)(lambda d=d: greet(row + d, me))

    @pl.when(row == 0)
    def _():
        def greet_line(r, _):
            greet(r, me)
            return 0

        lax.fori_loop(4, NR, greet_line, 0)

    expected = 14 + 4 * (source < row).astype(jnp.int32) + n_below + member + (row >= 4).astype(jnp.int32)

    for fetch in fetch_ints:
        fetch.wait()
    fetch_left.wait()

    count = left_count[0, 0]
    for k in range(4):
        slot = [left[:, s, k * 128 : (k + 1) * 128] for s in range(4)]
        for t in range(4):
            total = jnp.zeros((8, 128), jnp.float32)
            for s in range(4):
                hit = jnp.logical_and(left_index[0, 0, s] == t, s < count)
                total = jnp.where(hit, slot[s], total)
            strips[k, t] = total
    own_id[...] = jnp.full((1, 128), right_index[0, 0], jnp.int32)
    pl.semaphore_wait(barrier, expected)

    def spread(k):
        return pltpu.make_async_remote_copy(
            src_ref=strips.at[k],
            dst_ref=staged.at[k],
            send_sem=s1.at[k],
            recv_sem=r1.at[k],
            device_id=(row, on_line(2 * k + parity)),
            device_id_type=MESH,
        )

    def tell(sem, r, c):
        pl.semaphore_signal(sem, inc=1, device_id=(r, c), device_id_type=MESH)

    @pl.when(source < row)
    def _():
        for q in range(4):
            tell(ready, source, sender(q))

    for k in range(1, 4):
        spread(k).start()
    pl.when(parity == 1)(lambda: spread(0).start())

    @pl.when(parity == 0)
    def _():
        staged[0] = strips[0]

    for d in range(1, 8):
        tell(plane_ready, row, on_line(d))
    for d in range(1, 4):
        pl.when(member >= d)(lambda d=d: tell(near_ready, row - d, me))

    def to_plane(k):
        return pltpu.make_async_remote_copy(
            src_ref=staged.at[k],
            dst_ref=tiles.at[pl.ds(quarter * 4, 4)],
            send_sem=s2.at[k],
            recv_sem=r2,
            device_id=holder(k),
            device_id_type=MESH,
        )

    here = jnp.logical_and(hold_x == x, hold_core == core)
    kept = [jnp.logical_and(here, planes[k] == row) for k in range(4)]
    sent = [jnp.logical_not(keep) for keep in kept]

    def keep_here(k):
        return pltpu.make_async_copy(staged.at[k], tiles.at[pl.ds(quarter * 4, 4)], r2)

    def pass_on(k):
        pl.when(jnp.logical_and(sent[k], planes[k] <= row))(lambda: to_plane(k).start())
        pl.when(kept[k])(lambda: keep_here(k).start())

    def send_id(d):
        return pltpu.make_async_remote_copy(
            src_ref=own_id,
            dst_ref=ids.at[y, lax.rem(me, 8)],
            send_sem=si,
            recv_sem=ri,
            device_id=(row, y * 8 + lax.rem(me + d, 8)),
            device_id_type=MESH,
        )

    def send_ids(d):
        return pltpu.make_async_remote_copy(
            src_ref=ids.at[y],
            dst_ref=ids.at[y],
            send_sem=sj,
            recv_sem=rj,
            device_id=(row, on_line(d)),
            device_id_type=MESH,
        )

    for d in range(1, 8):
        send_id(d).start()
    ids[y, lax.rem(me, 8)] = own_id[...]
    pl.when(parity == 1)(lambda: spread(0).wait_recv())
    pass_on(0)
    wait_for(ids.at[0, pl.ds(0, 7)], ri)
    for d in range(1, 8):
        send_ids(d).start()
    for k in (1, 3, 2):
        spread(k).wait_recv()
        pass_on(k)

    @pl.when(n_above > 0)
    def _():
        pl.semaphore_wait(ready, n_above)
        for k in range(4):
            pl.when(planes[k] > row)(lambda k=k: to_plane(k).start())

    wait_for(ids.at[pl.ds(0, 7)], rj)
    read = pltpu.make_async_copy(ids, ids_s, sem_ids)
    read.start()
    read.wait()
    wait_for(tiles, r2)
    pl.semaphore_wait(plane_ready, 7)

    slot_here = chunk * 16 + source

    def send_tile(c, d):
        picked[d] = tiles[ids_s[c // 8, lax.rem(c, 8), 0, 0]]
        pltpu.make_async_remote_copy(
            src_ref=picked.at[d],
            dst_ref=panel.at[slot_here],
            send_sem=s3,
            recv_sem=r3.at[source // 8],
            device_id=(row, c),
            device_id_type=MESH,
        ).start()

    for n in range(16):
        to_core, d = n // 8, (4, 3, 5, 2, 6, 1, 7, 0)[n % 8]

        def send_group(i, _, n=n, to_core=to_core, d=d):
            c = lax.rem(y + d, 8) * 8 + 2 * lax.rem(x + i, 4) + to_core
            pl.when(c != me)(lambda: send_tile(c, n * 4 + i))
            return 0

        lax.fori_loop(0, 4, send_group, 0)

    panel[slot_here] = tiles[ids_s[y, lax.rem(me, 8), 0, 0]]
    fetch_right.wait()

    group = row // 4
    first = group * 4 + group // 2 * 2

    def gather_near(h):
        return pltpu.make_async_remote_copy(
            src_ref=part.at[h],
            dst_ref=near.at[member],
            send_sem=s4.at[h],
            recv_sem=r4,
            device_id=(first + h, me),
            device_id_type=MESH,
        )

    def give(r):
        return pltpu.make_async_remote_copy(
            src_ref=result.at[r],
            dst_ref=mine,
            send_sem=s6,
            recv_sem=r6,
            device_id=(r, me),
            device_id_type=MESH,
        )

    def multiply(h):
        pl.when(source // 8 == h)(lambda: wait_for(panel.at[pl.ds(0, 31)], r3.at[h]))
        pl.when(source // 8 != h)(lambda: wait_for(panel.at[pl.ds(0, 32)], r3.at[h]))
        a = jnp.concatenate([panel[pl.ds(k * 16 + h * 8, 8)].reshape(64, 128) for k in range(4)], axis=1)
        total = jnp.dot(a, right[...], precision=lax.Precision.HIGHEST, preferred_element_type=jnp.float32)
        part[h] = total.reshape(8, 8, 128)
        pl.when(row != first + h)(lambda: gather_near(h).start())

        @pl.when(row == first + h)
        def _():
            near[member] = part[h]

    pl.when(member < 3)(lambda: pl.semaphore_wait(near_ready, 3 - member))
    own_half = row // 8
    multiply(own_half)
    multiply(1 - own_half)
    for h in range(2):

        @pl.when(row == first + h)
        def _(h=h):
            wait_for(near.at[pl.ds(0, 3)], r4)
            half[...] = near[0] + near[1] + near[2] + near[3]

    gather_far = pltpu.make_async_remote_copy(
        src_ref=half,
        dst_ref=far.at[group * 2 + row - first],
        send_sem=s5,
        recv_sem=r5,
        device_id=(0, me),
        device_id_type=MESH,
    )
    holds = jnp.logical_and(row != 0, jnp.logical_or(row == first, row == first + 1))
    pl.when(holds)(lambda: gather_far.start())

    @pl.when(row != 0)
    def _():
        wait_for(mine, r6)
        out[...] = mine[...]

    @pl.when(row == 0)
    def _():
        far[0] = half[...]
        wait_for(far.at[pl.ds(0, 7)], r5)
        product = jnp.sum(far[...].reshape(4, 16, 8, 128), axis=0)
        squared = product * product
        colsum = jnp.sum(jnp.sum(squared, axis=0), axis=0, keepdims=True)
        result[...] = squared * (128.0 / (colsum + 1e-06))[None]
        for r in range(1, NR):
            give(r).start()
        out[...] = result[0]
        wait_for(result.at[pl.ds(0, NR - 1)], s6)

    pl.when(holds)(lambda: gather_far.wait_send())
    for h in range(2):
        pl.when(row != first + h)(lambda h=h: gather_near(h).wait_send())
    for k in range(1, 4):
        spread(k).wait_send()
    pl.when(parity == 1)(lambda: spread(0).wait_send())
    for k in range(4):
        pl.when(sent[k])(lambda k=k: to_plane(k).wait_send())
    wait_for(ids.at[0, pl.ds(0, 7)], si)
    wait_for(ids.at[pl.ds(0, 7)], sj)
    wait_for(picked.at[pl.ds(1, NC - 1)], s3)


def body(left_tiles, left_index, left_count, right_tiles, right_index):
    f32, i32 = jnp.float32, jnp.int32
    dma = pltpu.SemaphoreType.DMA
    return pl.pallas_call(
        kernel,
        out_shape=jax.ShapeDtypeStruct((8, 128), f32),
        in_specs=[pl.BlockSpec(memory_space=pltpu.HBM)] * 5,
        out_specs=pl.BlockSpec(memory_space=pltpu.VMEM),
        scratch_shapes=[
            pltpu.VMEM((8, 4, 512), f32),
            pltpu.SMEM((1, 1, 4), i32),
            pltpu.SMEM((1, 1), i32),
            pltpu.VMEM((512, 128), f32),
            pltpu.SMEM((1, 1), i32),
            pltpu.VMEM((4, 4, 8, 128), f32),
            pltpu.VMEM((4, 4, 8, 128), f32),
            pltpu.VMEM((16, 8, 128), f32),
            pltpu.VMEM((NC, 8, 128), f32),
            pltpu.VMEM((NC, 8, 128), f32),
            pltpu.VMEM((1, 128), i32),
            pltpu.VMEM((8, 8, 1, 128), i32),
            pltpu.SMEM((8, 8, 1, 128), i32),
            pltpu.VMEM((2, 8, 8, 128), f32),
            pltpu.VMEM((4, 8, 8, 128), f32),
            pltpu.VMEM((8, 8, 128), f32),
            pltpu.VMEM((8, 8, 8, 128), f32),
            pltpu.VMEM((NR, 8, 128), f32),
            pltpu.VMEM((8, 128), f32),
            dma, dma((3,)), dma, dma, dma((4,)), dma((4,)), dma((4,)),
        ]
        + [dma] * 6
        + [dma((2,)), dma((2,))]
        + [dma] * 5
        + [pltpu.SemaphoreType.REGULAR] * 3,
        compiler_params=pltpu.CompilerParams(
            collective_id=0, has_side_effects=True, vmem_limit_bytes=55168 << 10
        ),
    )(left_tiles, left_index, left_count, right_tiles, right_index)


def solution(mesh):
    return jax.shard_map(
        body,
        mesh=mesh,
        in_specs=(
            P("row", "col", None),
            P("row", "col", None),
            P("row", "col"),
            P("row", "col"),
            P("row", "col"),
        ),
        out_specs=P("row", "col"),
        check_vma=False,
    )
```

```python
import jax
import jax.numpy as jnp
from jax import lax
from jax.experimental import pallas as pl
from jax.experimental.pallas import tpu as pltpu
from jax.sharding import PartitionSpec as P

MESH = pl.DeviceIdType.MESH
NR, NC = 16, 64


def wait_for(ref, sem):
    pltpu.make_async_copy(ref, ref, sem).wait()


def kernel(
    left_hbm, index_hbm, count_hbm, right_hbm, own_hbm, out,
    left, left_index, left_count, right, right_index,
    strips, staged, tiles, picked, panel, own_id, ids, ids_s, part, near, half, far, result, mine,
    sem_left, sem_int, sem_right, sem_ids, s1, r1, s2, r2, si, ri, sj, rj, s3, r3, s4, r4, s5, r5, s6, r6, ready, plane_ready, near_ready,
):
    row, me = lax.axis_index("row"), lax.axis_index("col")
    barrier = pltpu.get_barrier_semaphore()

    def greet(r, c):
        pl.semaphore_signal(barrier, inc=1, device_id=(r, c), device_id_type=MESH)

    ints = ((index_hbm, left_index), (count_hbm, left_count), (own_hbm, right_index))
    fetch_ints = [pltpu.make_async_copy(a, b, sem_int.at[i]) for i, (a, b) in enumerate(ints)]
    fetch_left = pltpu.make_async_copy(left_hbm, left, sem_left)
    fetch_right = pltpu.make_async_copy(right_hbm, right, sem_right)
    for fetch in fetch_ints:
        fetch.start()
    fetch_left.start()
    fetch_right.start()

    y, x, core = me // 8, lax.rem(me // 2, 4), lax.rem(me, 2)
    quarter = lax.rem(me, 4)
    offset = lax.rem(y - row // 2 + 8, 8)
    chunk = offset // 2
    source = x // 2 + 2 * lax.rem(x, 2) + 4 * core + 8 * lax.rem(offset, 2)
    parity = row // 8
    hold_x, hold_core = 2 * lax.rem(row, 2) + lax.rem(row // 2, 2), lax.rem(row // 4, 2)

    planes = [2 * lax.rem(y - 2 * k - parity + 8, 8) + x // 2 for k in range(4)]
    above = [(p > row).astype(jnp.int32) for p in planes]
    below = [(p < row).astype(jnp.int32) for p in planes]
    n_above = above[0] + above[1] + above[2] + above[3]
    n_below = below[0] + below[1] + below[2] + below[3]
    member = lax.rem(row, 4)

    def on_line(d):
        return lax.rem(y + d, 8) * 8 + lax.rem(me, 8)

    def sender(q):
        return y * 8 + lax.rem(row, 2) * 4 + q

    def holder(k):
        return planes[k], y * 8 + hold_x * 2 + hold_core

    for d in range(1, 8):
        greet(row, on_line(d))
    for d in range(1, 8):
        greet(row, y * 8 + lax.rem(me + d, 8))

    @pl.when(source > row)
    def _():
        for q in range(4):
            greet(source, sender(q))

    for k in range(4):
        pl.when(planes[k] > row)(lambda k=k: greet(*holder(k)))
    for d in range(1, 4):
        pl.when(member + d < 4)(lambda d=d: greet(row + d, me))

    @pl.when(row == 0)
    def _():
        def greet_line(r, _):
            greet(r, me)
            return 0

        lax.fori_loop(4, NR, greet_line, 0)

    expected = 14 + 4 * (source < row).astype(jnp.int32) + n_below + member + (row >= 4).astype(jnp.int32)

    for fetch in fetch_ints:
        fetch.wait()
    fetch_left.wait()

    count = left_count[0, 0]
    for k in range(4):
        slot = [left[:, s, k * 128 : (k + 1) * 128] for s in range(4)]
        for t in range(4):
            total = jnp.zeros((8, 128), jnp.float32)
            for s in range(4):
                hit = jnp.logical_and(left_index[0, 0, s] == t, s < count)
                total = jnp.where(hit, slot[s], total)
            strips[k, t] = total
    own_id[...] = jnp.full((1, 128), right_index[0, 0], jnp.int32)
    pl.semaphore_wait(barrier, expected)

    def spread(k):
        return pltpu.make_async_remote_copy(
            src_ref=strips.at[k],
            dst_ref=staged.at[k],
            send_sem=s1.at[k],
            recv_sem=r1.at[k],
            device_id=(row, on_line(2 * k + parity)),
            device_id_type=MESH,
        )

    def tell(sem, r, c):
        pl.semaphore_signal(sem, inc=1, device_id=(r, c), device_id_type=MESH)

    @pl.when(source < row)
    def _():
        for q in range(4):
            tell(ready, source, sender(q))

    for k in range(1, 4):
        spread(k).start()
    pl.when(parity == 1)(lambda: spread(0).start())

    @pl.when(parity == 0)
    def _():
        staged[0] = strips[0]

    for d in range(1, 8):
        tell(plane_ready, row, on_line(d))
    for d in range(1, 4):
        pl.when(member >= d)(lambda d=d: tell(near_ready, row - d, me))

    def to_plane(k):
        return pltpu.make_async_remote_copy(
            src_ref=staged.at[k],
            dst_ref=tiles.at[pl.ds(quarter * 4, 4)],
            send_sem=s2.at[k],
            recv_sem=r2,
            device_id=holder(k),
            device_id_type=MESH,
        )

    here = jnp.logical_and(hold_x == x, hold_core == core)
    kept = [jnp.logical_and(here, planes[k] == row) for k in range(4)]
    sent = [jnp.logical_not(keep) for keep in kept]

    def keep_here(k):
        return pltpu.make_async_copy(staged.at[k], tiles.at[pl.ds(quarter * 4, 4)], r2)

    def pass_on(k):
        pl.when(jnp.logical_and(sent[k], planes[k] <= row))(lambda: to_plane(k).start())
        pl.when(kept[k])(lambda: keep_here(k).start())

    def send_id(d):
        return pltpu.make_async_remote_copy(
            src_ref=own_id,
            dst_ref=ids.at[y, lax.rem(me, 8)],
            send_sem=si,
            recv_sem=ri,
            device_id=(row, y * 8 + lax.rem(me + d, 8)),
            device_id_type=MESH,
        )

    def send_ids(d):
        return pltpu.make_async_remote_copy(
            src_ref=ids.at[y],
            dst_ref=ids.at[y],
            send_sem=sj,
            recv_sem=rj,
            device_id=(row, on_line(d)),
            device_id_type=MESH,
        )

    for d in range(1, 8):
        send_id(d).start()
    ids[y, lax.rem(me, 8)] = own_id[...]
    pl.when(parity == 1)(lambda: spread(0).wait_recv())
    pass_on(0)
    wait_for(ids.at[0, pl.ds(0, 7)], ri)
    for d in range(1, 8):
        send_ids(d).start()
    for k in (1, 3, 2):
        spread(k).wait_recv()
        pass_on(k)

    @pl.when(n_above > 0)
    def _():
        pl.semaphore_wait(ready, n_above)
        for k in range(4):
            pl.when(planes[k] > row)(lambda k=k: to_plane(k).start())

    wait_for(ids.at[pl.ds(0, 7)], rj)
    read = pltpu.make_async_copy(ids, ids_s, sem_ids)
    read.start()
    read.wait()
    wait_for(tiles, r2)
    pl.semaphore_wait(plane_ready, 7)

    slot_here = chunk * 16 + source

    def send_tile(c, d):
        picked[d] = tiles[ids_s[c // 8, lax.rem(c, 8), 0, 0]]
        pltpu.make_async_remote_copy(
            src_ref=picked.at[d],
            dst_ref=panel.at[slot_here],
            send_sem=s3,
            recv_sem=r3.at[source // 8],
            device_id=(row, c),
            device_id_type=MESH,
        ).start()

    for n in range(16):
        to_core, d = n // 8, (4, 3, 5, 2, 6, 1, 7, 0)[n % 8]

        def send_group(i, _, n=n, to_core=to_core, d=d):
            c = lax.rem(y + d, 8) * 8 + 2 * lax.rem(x + i, 4) + to_core
            if d == 0:
                pl.when(c != me)(lambda: send_tile(c, n * 4 + i))
            else:
                send_tile(c, n * 4 + i)
            return 0

        lax.fori_loop(0, 4, send_group, 0)

    panel[slot_here] = tiles[ids_s[y, lax.rem(me, 8), 0, 0]]
    fetch_right.wait()

    group = row // 4
    first = group * 4 + group // 2 * 2

    def gather_near(h):
        return pltpu.make_async_remote_copy(
            src_ref=part.at[h],
            dst_ref=near.at[member],
            send_sem=s4.at[h],
            recv_sem=r4,
            device_id=(first + h, me),
            device_id_type=MESH,
        )

    def give(r):
        return pltpu.make_async_remote_copy(
            src_ref=result.at[r],
            dst_ref=mine,
            send_sem=s6,
            recv_sem=r6,
            device_id=(r, me),
            device_id_type=MESH,
        )

    def multiply(h):
        pl.when(source // 8 == h)(lambda: wait_for(panel.at[pl.ds(0, 31)], r3.at[h]))
        pl.when(source // 8 != h)(lambda: wait_for(panel.at[pl.ds(0, 32)], r3.at[h]))
        a = jnp.concatenate([panel[pl.ds(k * 16 + h * 8, 8)].reshape(64, 128) for k in range(4)], axis=1)
        total = jnp.dot(a, right[...], precision=lax.Precision.HIGHEST, preferred_element_type=jnp.float32)
        part[h] = total.reshape(8, 8, 128)
        pl.when(row != first + h)(lambda: gather_near(h).start())

        @pl.when(row == first + h)
        def _():
            near[member] = part[h]

    pl.when(member < 3)(lambda: pl.semaphore_wait(near_ready, 3 - member))
    own_half = row // 8
    multiply(own_half)
    multiply(1 - own_half)
    for h in range(2):

        @pl.when(row == first + h)
        def _(h=h):
            wait_for(near.at[pl.ds(0, 3)], r4)
            half[...] = near[0] + near[1] + near[2] + near[3]

    gather_far = pltpu.make_async_remote_copy(
        src_ref=half,
        dst_ref=far.at[group * 2 + row - first],
        send_sem=s5,
        recv_sem=r5,
        device_id=(0, me),
        device_id_type=MESH,
    )
    holds = jnp.logical_and(row != 0, jnp.logical_or(row == first, row == first + 1))
    pl.when(holds)(lambda: gather_far.start())

    @pl.when(row != 0)
    def _():
        wait_for(mine, r6)
        out[...] = mine[...]

    @pl.when(row == 0)
    def _():
        far[0] = half[...]
        wait_for(far.at[pl.ds(0, 7)], r5)
        product = jnp.sum(far[...].reshape(4, 16, 8, 128), axis=0)
        squared = product * product
        colsum = jnp.sum(jnp.sum(squared, axis=0), axis=0, keepdims=True)
        result[...] = squared * (128.0 / (colsum + 1e-06))[None]
        for r in range(1, NR):
            give(r).start()
        out[...] = result[0]
        wait_for(result.at[pl.ds(0, NR - 1)], s6)

    pl.when(holds)(lambda: gather_far.wait_send())
    for h in range(2):
        pl.when(row != first + h)(lambda h=h: gather_near(h).wait_send())
    for k in range(1, 4):
        spread(k).wait_send()
    pl.when(parity == 1)(lambda: spread(0).wait_send())
    for k in range(4):
        pl.when(sent[k])(lambda k=k: to_plane(k).wait_send())
    wait_for(ids.at[0, pl.ds(0, 7)], si)
    wait_for(ids.at[pl.ds(0, 7)], sj)
    wait_for(picked.at[pl.ds(1, NC - 1)], s3)


def body(left_tiles, left_index, left_count, right_tiles, right_index):
    f32, i32 = jnp.float32, jnp.int32
    dma = pltpu.SemaphoreType.DMA
    return pl.pallas_call(
        kernel,
        out_shape=jax.ShapeDtypeStruct((8, 128), f32),
        in_specs=[pl.BlockSpec(memory_space=pltpu.HBM)] * 5,
        out_specs=pl.BlockSpec(memory_space=pltpu.VMEM),
        scratch_shapes=[
            pltpu.VMEM((8, 4, 512), f32),
            pltpu.SMEM((1, 1, 4), i32),
            pltpu.SMEM((1, 1), i32),
            pltpu.VMEM((512, 128), f32),
            pltpu.SMEM((1, 1), i32),
            pltpu.VMEM((4, 4, 8, 128), f32),
            pltpu.VMEM((4, 4, 8, 128), f32),
            pltpu.VMEM((16, 8, 128), f32),
            pltpu.VMEM((NC, 8, 128), f32),
            pltpu.VMEM((NC, 8, 128), f32),
            pltpu.VMEM((1, 128), i32),
            pltpu.VMEM((8, 8, 1, 128), i32),
            pltpu.SMEM((8, 8, 1, 128), i32),
            pltpu.VMEM((2, 8, 8, 128), f32),
            pltpu.VMEM((4, 8, 8, 128), f32),
            pltpu.VMEM((8, 8, 128), f32),
            pltpu.VMEM((8, 8, 8, 128), f32),
            pltpu.VMEM((NR, 8, 128), f32),
            pltpu.VMEM((8, 128), f32),
            dma, dma((3,)), dma, dma, dma((4,)), dma((4,)), dma((4,)),
        ]
        + [dma] * 6
        + [dma((2,)), dma((2,))]
        + [dma] * 5
        + [pltpu.SemaphoreType.REGULAR] * 3,
        compiler_params=pltpu.CompilerParams(
            collective_id=0, has_side_effects=True, vmem_limit_bytes=55168 << 10
        ),
    )(left_tiles, left_index, left_count, right_tiles, right_index)


def solution(mesh):
    return jax.shard_map(
        body,
        mesh=mesh,
        in_specs=(
            P("row", "col", None),
            P("row", "col", None),
            P("row", "col"),
            P("row", "col"),
            P("row", "col"),
        ),
        out_specs=P("row", "col"),
        check_vma=False,
    )
```
